32 devices in a mesh: dp: 32 (over z, y, x, core).
Axes of the slice: x: 2, y: 2, z: 4, core: 2. Of those that a mesh axis runs over, the one named last changes fastest.
Arguments:
- picture_embeddings_raw: float32 [8192, 1152], P('dp'), may hold values from -0.18 to 0.18
- caption_embeddings_raw: float32 [8192, 1152], P('dp'), may hold values from -0.18 to 0.18
- sharpness_array: float32 [1], replicated, may hold values from 5 to 15
- offset_term_array: float32 [1], replicated, may hold values from -4 to -1
Outputs:
- row_loss: float32 [8192], P('dp')
- grad_image: float32 [8192, 1152], P('dp')
- grad_text: float32 [8192, 1152], P('dp')
The draws below stay inside these ranges and needn't reach their ends.
All inputs are finite; a program needn't handle non-finite values.
Results may differ from the reference program's by a relative error of at most 0.003.
Values may be sent and summed in bfloat16 or wider, within the bound.
A program may use at most 64 MiB of HBM per device.

```python
import jax
import jax.numpy as jnp
from jax import lax

D = 1152
ROWS = 256
STEPS = 8
BATCH = 8192
N_DP = 32


def level_of(stream_key, dims, split, smallest, largest):
    level, own = 1.0, jax.random.fold_in(stream_key, 6)
    for dim, shards_of in split:
        heights = jnp.exp(jax.random.uniform(jax.random.fold_in(own, dim), (shards_of,), jnp.float32, smallest / len(split), largest / len(split)))
        level = level * jnp.repeat(heights, dims[dim] // shards_of).reshape([-1 if axis == dim else 1 for axis in range(len(dims))])
    return level


def noise(key, shape, spread, limit, pieces=(), kind=jnp.bfloat16):
    values = spread * jax.random.normal(key, shape, jnp.float32)
    if pieces:
        values = values * level_of(key, shape, pieces, -0.22, 0.18)
    return jnp.clip(values, -limit, limit).astype(kind)


def setup_inputs(seed: int = 0) -> dict:
    key_list = jax.random.split(jax.random.key(seed), 5)
    return {
        "picture_embeddings_raw": noise(key_list[0], (BATCH, D), 0.03, 0.18, ((0, 32),), jnp.float32),
        "caption_embeddings_raw": noise(key_list[1], (BATCH, D), 0.03, 0.18, ((0, 32),), jnp.float32),
        "sharpness_array": jnp.clip(jax.random.uniform(key_list[2], (1,), jnp.float32, 5.0, 15.0), 5.0, 15.0),
        "offset_term_array": jnp.clip(jax.random.uniform(key_list[3], (1,), jnp.float32, -4.0, -1.0), -4.0, -1.0),
    }


epsilon = 1e-06

def unit_rows(values):
    radius = jnp.sqrt(lax.optimization_barrier(jnp.sum(values * values, axis=-1, keepdims=True)) + epsilon)
    return (values / radius, radius)

def back_rows(grad_unit, unit, radius):
    inner = lax.optimization_barrier(jnp.sum(unit * grad_unit, axis=-1, keepdims=True))
    return (grad_unit - unit * inner) / radius

def reference(picture_embeddings_raw, caption_embeddings_raw, sharpness_array, offset_term_array):
    image_unit_vectors, img_radius = unit_rows(picture_embeddings_raw)
    txt_unit, txt_radius = unit_rows(caption_embeddings_raw)
    txt_round = lax.optimization_barrier(txt_unit.astype(jnp.bfloat16)).astype(jnp.float32)
    picture_tiles = image_unit_vectors.reshape(N_DP, ROWS, D)
    txt_blocks = txt_round.reshape(N_DP, ROWS, D)
    sharpness_multiplier = sharpness_array[0]
    additive_offset_term = offset_term_array[0]
    diagonal_ones = jnp.eye(ROWS, dtype=jnp.float32)
    loss_total = jnp.zeros((N_DP, ROWS), jnp.float32)
    picture_derivative_sum = jnp.zeros((N_DP, ROWS, D), jnp.float32)
    grad_txt = jnp.zeros((N_DP, ROWS, D), jnp.float32)
    half_steps = STEPS // 2
    for offset in range(-half_steps, half_steps):
        neighbor_shard_index = jnp.roll(txt_blocks, -offset, axis=0)
        matching_scores = sharpness_multiplier * jnp.einsum('rzq,rbq->rzb', picture_tiles, neighbor_shard_index, precision=lax.Precision.HIGHEST) + additive_offset_term
        if offset == 0:
            positive = diagonal_ones
        else:
            positive = jnp.zeros((ROWS, ROWS), jnp.float32)
        loss_total = loss_total + lax.optimization_barrier(jnp.sum(jax.nn.softplus(matching_scores) - positive * matching_scores, axis=-1))
        match_weight_factor = jax.nn.sigmoid(matching_scores) - positive
        picture_derivative_sum = picture_derivative_sum + sharpness_multiplier * jnp.einsum('rbk,rkx->rbx', match_weight_factor, neighbor_shard_index, precision=lax.Precision.HIGHEST)
        caption_piece = sharpness_multiplier * jnp.einsum('nky,nku->nyu', match_weight_factor, picture_tiles, precision=lax.Precision.HIGHEST)
        grad_txt = grad_txt + jnp.roll(caption_piece, offset, axis=0)
    row_loss = loss_total.reshape(BATCH) / (STEPS * ROWS)
    grad_image = back_rows(picture_derivative_sum.reshape(BATCH, D), image_unit_vectors, img_radius)
    grad_text = back_rows(grad_txt.reshape(BATCH, D), txt_unit, txt_radius)
    return (row_loss, grad_image, grad_text)
```

```python
import functools

import jax
import jax.numpy as jnp
from jax import lax
from jax.experimental import pallas as pl
from jax.experimental.pallas import tpu as pltpu
from jax.sharding import PartitionSpec as P

STEPS = 8


epsilon = 1e-06


def shifted(value, axis, by):
    size = lax.axis_size(axis)
    return lax.ppermute(value, axis, [(i, (i + by) % size) for i in range(size)])


def unit_rows(values):
    radius = jnp.sqrt(jnp.sum(values * values, axis=-1, keepdims=True) + epsilon)
    return (values / radius, radius)


def back_rows(grad_unit, unit, radius):
    inner = jnp.sum(unit * grad_unit, axis=-1, keepdims=True)
    return (grad_unit - unit * inner) / radius


def per_device(picture_embeddings_raw, caption_embeddings_raw, sharpness_array, offset_term_array):
    row_count = picture_embeddings_raw.shape[0]
    step_total = STEPS
    half_steps = step_total // 2
    image_unit_vectors, img_radius = unit_rows(picture_embeddings_raw)
    txt_unit, txt_radius = unit_rows(caption_embeddings_raw)
    txt_send = txt_unit.astype(jnp.bfloat16)
    sharpness_multiplier = sharpness_array[0]
    additive_offset_term = offset_term_array[0]
    diagonal_ones = jnp.eye(row_count, dtype=jnp.float32)

    def labels(offset):
        if offset == 0:
            return diagonal_ones
        return jnp.zeros_like(diagonal_ones)

    chains = (-half_steps, 1, step_total)
    loss_total = jnp.zeros((row_count,), jnp.float32)
    picture_derivative_sum = jnp.zeros_like(image_unit_vectors)
    first_offset, direction, chain_steps = chains
    text_block = shifted(txt_send, "dp", -first_offset)
    carried = jnp.zeros_like(txt_unit)
    offset = first_offset
    for turn_index in range(chain_steps):
        offset = first_offset + direction * turn_index
        if turn_index > 0:
            text_block = shifted(text_block, "dp", -direction)
            carried = shifted(carried, "dp", -direction)
        neighbor_shard_index = text_block.astype(jnp.float32)
        matching_scores = (
            sharpness_multiplier
            * jnp.dot(image_unit_vectors, neighbor_shard_index.T, precision=lax.Precision.HIGHEST)
            + additive_offset_term
        )
        positive = labels(offset)
        loss_rows = jnp.sum(jax.nn.softplus(matching_scores) - positive * matching_scores, axis=1)
        match_weight_factor = jax.nn.sigmoid(matching_scores) - positive
        picture_piece = sharpness_multiplier * jnp.dot(
            match_weight_factor, neighbor_shard_index, precision=lax.Precision.HIGHEST
        )
        caption_piece = sharpness_multiplier * jnp.dot(
            match_weight_factor.T, image_unit_vectors, precision=lax.Precision.HIGHEST
        )
        loss_rows, picture_piece, caption_piece = (loss_rows, picture_piece, caption_piece)
        loss_total = loss_total + loss_rows
        picture_derivative_sum = picture_derivative_sum + picture_piece
        carried = carried + caption_piece
    text_total = shifted(carried, "dp", offset)
    row_loss = loss_total / (step_total * row_count)
    grad_image = back_rows(picture_derivative_sum, image_unit_vectors, img_radius)
    grad_text = back_rows(text_total, txt_unit, txt_radius)
    return (row_loss, grad_image, grad_text)


OWN, SIB, X, Y, Z, V, FAR, SIB_X, SIB_E, SIB_F = range(10)
SLOTS = 10
CHUNKS = 2
SENDS = 18


def tree_kernel(
    picture_ref, caption_ref, sharp_ref, offset_ref,
    loss_ref, grad_image_ref, grad_text_ref,
    txt, img, img_low, txt_sem, img_sem, send_sem,
):
    rows, width = picture_ref.shape
    part = rows // CHUNKS
    me = lax.axis_index("dp")
    total = lax.axis_size("dp")
    core = lax.rem(me, 2)
    x = lax.rem(me // 2, 2)
    y = lax.rem(me // 4, 2)
    corner = x == y
    plane = 8
    to_x = me + 2 - 4 * x
    to_y = me + 4 - 8 * y
    to_sib = me + 1 - 2 * core
    step = plane - 2 * plane * y
    z_out = lax.rem(me + step + total, total)
    z_in = lax.rem(me - step + total, total)
    skip_txt_z = jnp.logical_and(jnp.logical_and(x == 1, y == 1), core == 1)
    skip_img_z = jnp.logical_and(y == 0, core == 0)

    barrier = pltpu.get_barrier_semaphore()
    for peer in (to_x, to_y, to_sib, z_in):
        pl.semaphore_signal(barrier, inc=1, device_id=(peer,), device_id_type=pl.DeviceIdType.MESH)

    def copy(buf, sem, src, dst, chunk, number, target):
        at = pl.ds(chunk * part, part)
        return pltpu.make_async_remote_copy(
            src_ref=buf.at[src, at],
            dst_ref=buf.at[dst, at],
            send_sem=send_sem.at[number, chunk],
            recv_sem=sem.at[dst, chunk],
            device_id=(target,),
            device_id_type=pl.DeviceIdType.MESH,
        )

    def send_txt(src, dst, chunk, number, target):
        copy(txt, txt_sem, src, dst, chunk, number, target).start()

    def send_img(src, dst, chunk, number, target):
        copy(img, img_sem, src, dst, chunk, number, target).start()

    def wait_txt(dst, chunk):
        copy(txt, txt_sem, dst, dst, chunk, 0, to_sib).wait_recv()

    def wait_img(dst, chunk):
        copy(img, img_sem, dst, dst, chunk, 0, to_sib).wait_recv()

    def unit(values):
        radius = jnp.sqrt(jnp.sum(values * values, axis=-1, keepdims=True) + epsilon)
        return values / radius, radius

    chunks = range(CHUNKS)
    sharp = sharp_ref[0]
    shift = offset_ref[0]

    txt_unit, _ = unit(caption_ref[...])
    txt[OWN] = txt_unit.astype(jnp.bfloat16)
    pl.semaphore_wait(barrier, 4)
    for c in chunks:
        send_txt(OWN, Y, c, 0, to_y)
    img_unit, _ = unit(picture_ref[...])
    img_high = img_unit.astype(jnp.bfloat16)
    img[OWN] = img_high
    for c in chunks:
        send_img(OWN, X, c, 1, to_x)
    for c in chunks:
        send_txt(OWN, SIB, c, 2, to_sib)
        send_img(OWN, SIB, c, 3, to_sib)
    img_low[...] = (img_unit - img_high.astype(jnp.float32)).astype(jnp.bfloat16)

    loss_ref[...] = jnp.zeros_like(loss_ref)
    grad_image_ref[...] = jnp.zeros_like(grad_image_ref)
    grad_text_ref[...] = jnp.zeros_like(grad_text_ref)

    def product(a, b):
        return lax.dot_general(a, b, (((1,), (1,)), ((), ())), preferred_element_type=jnp.float32)

    def gather(coeff, block, acc):
        high = coeff.astype(jnp.bfloat16)
        low = (coeff - high.astype(jnp.float32)).astype(jnp.bfloat16)
        acc[...] += jnp.dot(high, block, preferred_element_type=jnp.float32) + jnp.dot(
            low, block, preferred_element_type=jnp.float32
        )

    def diagonal():
        shape = (rows, rows)
        return lax.broadcasted_iota(jnp.int32, shape, 0) == lax.broadcasted_iota(jnp.int32, shape, 1)

    def image_side(slot, diag=False):
        block = txt[slot]
        z = sharp * (product(img[OWN], block) + product(img_low[...], block)) + shift
        e = jnp.exp(-jnp.abs(z))
        loss = jnp.maximum(z, 0.0) + jnp.log1p(e)
        coeff = jnp.where(z >= 0, 1.0, e) / (1.0 + e)
        if diag:
            loss = loss - jnp.where(diagonal(), z, 0.0)
            coeff = coeff - jnp.where(diagonal(), 1.0, 0.0)
        loss_ref[...] += jnp.sum(loss, axis=1, keepdims=True)
        gather(coeff, block, grad_image_ref)

    def text_side(slot, diag=False):
        block = img[slot]
        z = sharp * product(txt[OWN], block) + shift
        e = jnp.exp(-jnp.abs(z))
        coeff = jnp.where(z >= 0, 1.0, e) / (1.0 + e)
        if diag:
            coeff = coeff - jnp.where(diagonal(), 1.0, 0.0)
        gather(coeff, block, grad_text_ref)

    image_side(OWN, True)
    text_side(OWN, True)

    for c in chunks:
        wait_txt(Y, c)
        @pl.when(jnp.logical_not(skip_txt_z))
        def _():
            send_txt(Y, Z, c, 4, z_out)
        wait_img(X, c)
        send_img(X, V, c, 5, to_y)
        send_img(X, SIB_X, c, 6, to_sib)
        send_img(OWN, Y, c, 7, to_y)
        send_txt(OWN, X, c, 8, to_x)

    for c in chunks:
        wait_txt(SIB, c)
        wait_img(SIB, c)
    image_side(SIB)
    text_side(SIB)
    text_side(X)

    early = lax.rem(y + core, 2) == 0
    for c in chunks:
        @pl.when(corner)
        def _():
            send_txt(Y, FAR, c, 9, to_x)
        @pl.when(jnp.logical_not(skip_txt_z))
        def _():
            wait_txt(Z, c)
        @pl.when(jnp.logical_not(corner))
        def _():
            send_txt(Z, FAR, c, 9, to_x)
        send_txt(lax.select(early, Y, Z), SIB_E, c, 10, to_sib)
        wait_img(V, c)
        @pl.when(corner)
        def _():
            send_img(V, FAR, c, 11, z_out)
        wait_img(Y, c)
        @pl.when(jnp.logical_not(skip_img_z))
        def _():
            send_img(Y, Z, c, 12, z_out)
        wait_txt(X, c)
        send_txt(X, SIB_X, c, 13, to_sib)

    for c in chunks:
        wait_img(SIB_X, c)
    text_side(SIB_X)
    image_side(X)
    image_side(lax.select(y == 0, Z, Y))
    for c in chunks:
        wait_txt(SIB_E, c)
        wait_txt(SIB_X, c)
    image_side(SIB_E)
    image_side(SIB_X)

    for c in chunks:
        @pl.when(jnp.logical_not(skip_img_z))
        def _():
            wait_img(Z, c)
        send_img(lax.select(early, Y, Z), SIB_E, c, 14, to_sib)
        wait_txt(FAR, c)
        send_txt(FAR, SIB_F, c, 15, to_sib)
        @pl.when(corner)
        def _():
            wait_img(FAR, c)
        send_img(lax.select(corner, FAR, V), SIB_F, c, 16, to_sib)
    text_side(lax.select(y == 0, Y, Z))
    image_side(FAR)
    text_side(lax.select(corner, FAR, V))
    for c in chunks:
        wait_img(SIB_E, c)
        wait_txt(SIB_F, c)
        wait_img(SIB_F, c)
    text_side(SIB_E)
    image_side(SIB_F)
    text_side(SIB_F)

    def back(raw, acc):
        own, radius = unit(raw)
        grad = sharp * acc
        inner = jnp.sum(own * grad, axis=-1, keepdims=True)
        return (grad - own * inner) / radius

    loss_ref[...] = loss_ref[...] * (1.0 / (STEPS * rows))
    grad_image_ref[...] = back(picture_ref[...], grad_image_ref[...])
    grad_text_ref[...] = back(caption_ref[...], grad_text_ref[...])

    def sent(number):
        for c in chunks:
            copy(txt, txt_sem, OWN, OWN, c, number, to_sib).wait_send()

    for number in (0, 1, 2, 3, 5, 6, 7, 8, 9, 10, 13, 14, 15, 16):
        sent(number)

    @pl.when(jnp.logical_not(skip_txt_z))
    def _():
        sent(4)

    @pl.when(corner)
    def _():
        sent(11)

    @pl.when(jnp.logical_not(skip_img_z))
    def _():
        sent(12)


def per_device_tree(picture, caption, sharpness, offset):
    rows, width = picture.shape
    vmem = pl.BlockSpec(memory_space=pltpu.VMEM)
    smem = pl.BlockSpec(memory_space=pltpu.SMEM)
    loss, grad_image, grad_text = pl.pallas_call(
        tree_kernel,
        out_shape=(
            jax.ShapeDtypeStruct((rows, 1), jnp.float32),
            jax.ShapeDtypeStruct((rows, width), jnp.float32),
            jax.ShapeDtypeStruct((rows, width), jnp.float32),
        ),
        in_specs=[vmem, vmem, smem, smem],
        out_specs=(vmem, vmem, vmem),
        scratch_shapes=[
            pltpu.VMEM((SLOTS, rows, width), jnp.bfloat16),
            pltpu.VMEM((SLOTS, rows, width), jnp.bfloat16),
            pltpu.VMEM((rows, width), jnp.bfloat16),
            pltpu.SemaphoreType.DMA((SLOTS, CHUNKS)),
            pltpu.SemaphoreType.DMA((SLOTS, CHUNKS)),
            pltpu.SemaphoreType.DMA((SENDS, CHUNKS)),
        ],
        compiler_params=pltpu.CompilerParams(
            collective_id=0, has_side_effects=True, vmem_limit_bytes=48 * 1024 * 1024
        ),
        cost_estimate=pl.CostEstimate(
            flops=14 * STEPS * rows * rows * width,
            bytes_accessed=16 * rows * width,
            transcendentals=4 * STEPS * rows * rows,
        ),
    )(picture, caption, sharpness, offset)
    return loss.reshape(rows), grad_image, grad_text


def solution(mesh):
    body = per_device_tree if mesh.shape["dp"] == 32 else per_device
    return jax.shard_map(
        body,
        mesh=mesh,
        in_specs=(P("dp", None), P("dp", None), P(), P()),
        out_specs=(P("dp"), P("dp", None), P("dp", None)),
        check_vma=False,
    )
```

```python
import functools

import jax
import jax.numpy as jnp
from jax import lax
from jax.experimental import pallas as pl
from jax.experimental.pallas import tpu as pltpu
from jax.sharding import PartitionSpec as P

STEPS = 8


epsilon = 1e-06


def shifted(value, axis, by):
    size = lax.axis_size(axis)
    return lax.ppermute(value, axis, [(i, (i + by) % size) for i in range(size)])


def unit_rows(values):
    radius = jnp.sqrt(jnp.sum(values * values, axis=-1, keepdims=True) + epsilon)
    return (values / radius, radius)


def back_rows(grad_unit, unit, radius):
    inner = jnp.sum(unit * grad_unit, axis=-1, keepdims=True)
    return (grad_unit - unit * inner) / radius


def per_device(picture_embeddings_raw, caption_embeddings_raw, sharpness_array, offset_term_array):
    row_count = picture_embeddings_raw.shape[0]
    step_total = STEPS
    half_steps = step_total // 2
    image_unit_vectors, img_radius = unit_rows(picture_embeddings_raw)
    txt_unit, txt_radius = unit_rows(caption_embeddings_raw)
    txt_send = txt_unit.astype(jnp.bfloat16)
    sharpness_multiplier = sharpness_array[0]
    additive_offset_term = offset_term_array[0]
    diagonal_ones = jnp.eye(row_count, dtype=jnp.float32)

    def labels(offset):
        if offset == 0:
            return diagonal_ones
        return jnp.zeros_like(diagonal_ones)

    chains = (-half_steps, 1, step_total)
    loss_total = jnp.zeros((row_count,), jnp.float32)
    picture_derivative_sum = jnp.zeros_like(image_unit_vectors)
    first_offset, direction, chain_steps = chains
    text_block = shifted(txt_send, "dp", -first_offset)
    carried = jnp.zeros_like(txt_unit)
    offset = first_offset
    for turn_index in range(chain_steps):
        offset = first_offset + direction * turn_index
        if turn_index > 0:
            text_block = shifted(text_block, "dp", -direction)
            carried = shifted(carried, "dp", -direction)
        neighbor_shard_index = text_block.astype(jnp.float32)
        matching_scores = (
            sharpness_multiplier
            * jnp.dot(image_unit_vectors, neighbor_shard_index.T, precision=lax.Precision.HIGHEST)
            + additive_offset_term
        )
        positive = labels(offset)
        loss_rows = jnp.sum(jax.nn.softplus(matching_scores) - positive * matching_scores, axis=1)
        match_weight_factor = jax.nn.sigmoid(matching_scores) - positive
        picture_piece = sharpness_multiplier * jnp.dot(
            match_weight_factor, neighbor_shard_index, precision=lax.Precision.HIGHEST
        )
        caption_piece = sharpness_multiplier * jnp.dot(
            match_weight_factor.T, image_unit_vectors, precision=lax.Precision.HIGHEST
        )
        loss_rows, picture_piece, caption_piece = (loss_rows, picture_piece, caption_piece)
        loss_total = loss_total + loss_rows
        picture_derivative_sum = picture_derivative_sum + picture_piece
        carried = carried + caption_piece
    text_total = shifted(carried, "dp", offset)
    row_loss = loss_total / (step_total * row_count)
    grad_image = back_rows(picture_derivative_sum, image_unit_vectors, img_radius)
    grad_text = back_rows(text_total, txt_unit, txt_radius)
    return (row_loss, grad_image, grad_text)


OWN, SIB, X, Y, Z, V, FAR, SIB_X, SIB_E, SIB_F = range(10)
SLOTS = 10
CHUNKS = 2
SENDS = 18


def tree_kernel(
    picture_ref, caption_ref, sharp_ref, offset_ref,
    loss_ref, grad_image_ref, grad_text_ref,
    txt, img, img_low, txt_sem, img_sem, send_sem,
):
    rows, width = picture_ref.shape
    part = rows // CHUNKS
    me = lax.axis_index("dp")
    total = lax.axis_size("dp")
    core = lax.rem(me, 2)
    x = lax.rem(me // 2, 2)
    y = lax.rem(me // 4, 2)
    corner = x == y
    plane = 8
    to_x = me + 2 - 4 * x
    to_y = me + 4 - 8 * y
    to_sib = me + 1 - 2 * core
    step = plane - 2 * plane * y
    z_out = lax.rem(me + step + total, total)
    z_in = lax.rem(me - step + total, total)
    skip_txt_z = jnp.logical_and(jnp.logical_and(x == 1, y == 1), core == 1)
    skip_img_z = jnp.logical_and(y == 0, core == 0)

    barrier = pltpu.get_barrier_semaphore()
    for peer in (to_x, to_y, to_sib, z_in):
        pl.semaphore_signal(barrier, inc=1, device_id=(peer,), device_id_type=pl.DeviceIdType.MESH)

    def copy(buf, sem, src, dst, chunk, number, target):
        at = pl.ds(chunk * part, part)
        return pltpu.make_async_remote_copy(
            src_ref=buf.at[src, at],
            dst_ref=buf.at[dst, at],
            send_sem=send_sem.at[number, chunk],
            recv_sem=sem.at[dst, chunk],
            device_id=(target,),
            device_id_type=pl.DeviceIdType.MESH,
        )

    def send_txt(src, dst, chunk, number, target):
        copy(txt, txt_sem, src, dst, chunk, number, target).start()

    def send_img(src, dst, chunk, number, target):
        copy(img, img_sem, src, dst, chunk, number, target).start()

    def wait_txt(dst, chunk):
        copy(txt, txt_sem, dst, dst, chunk, 0, to_sib).wait_recv()

    def wait_img(dst, chunk):
        copy(img, img_sem, dst, dst, chunk, 0, to_sib).wait_recv()

    def unit(values):
        radius = jnp.sqrt(jnp.sum(values * values, axis=-1, keepdims=True) + epsilon)
        return values / radius, radius

    chunks = range(CHUNKS)
    sharp = sharp_ref[0]
    shift = offset_ref[0]

    txt_unit, _ = unit(caption_ref[...])
    txt[OWN] = txt_unit.astype(jnp.bfloat16)
    pl.semaphore_wait(barrier, 4)
    for c in chunks:
        send_txt(OWN, Y, c, 0, to_y)
    img_unit, _ = unit(picture_ref[...])
    img_high = img_unit.astype(jnp.bfloat16)
    img[OWN] = img_high
    for c in chunks:
        send_img(OWN, X, c, 1, to_x)
    for c in chunks:
        send_txt(OWN, X, c, 8, to_x)

    @pl.when(corner)
    def _():
        for c in chunks:
            send_img(OWN, Y, c, 7, to_y)

    for c in chunks:
        send_txt(OWN, SIB, c, 2, to_sib)
        send_img(OWN, SIB, c, 3, to_sib)
    img_low[...] = (img_unit - img_high.astype(jnp.float32)).astype(jnp.bfloat16)

    loss_ref[...] = jnp.zeros_like(loss_ref)
    grad_image_ref[...] = jnp.zeros_like(grad_image_ref)
    grad_text_ref[...] = jnp.zeros_like(grad_text_ref)

    def product(a, b):
        return lax.dot_general(a, b, (((1,), (1,)), ((), ())), preferred_element_type=jnp.float32)

    def gather(coeff, block, acc):
        high = coeff.astype(jnp.bfloat16)
        low = (coeff - high.astype(jnp.float32)).astype(jnp.bfloat16)
        acc[...] += jnp.dot(high, block, preferred_element_type=jnp.float32) + jnp.dot(
            low, block, preferred_element_type=jnp.float32
        )

    def diagonal():
        shape = (rows, rows)
        return lax.broadcasted_iota(jnp.int32, shape, 0) == lax.broadcasted_iota(jnp.int32, shape, 1)

    def image_side(slot, diag=False):
        block = txt[slot]
        z = sharp * (product(img[OWN], block) + product(img_low[...], block)) + shift
        e = jnp.exp(-jnp.abs(z))
        loss = jnp.maximum(z, 0.0) + jnp.log1p(e)
        coeff = jnp.where(z >= 0, 1.0, e) / (1.0 + e)
        if diag:
            loss = loss - jnp.where(diagonal(), z, 0.0)
            coeff = coeff - jnp.where(diagonal(), 1.0, 0.0)
        loss_ref[...] += jnp.sum(loss, axis=1, keepdims=True)
        gather(coeff, block, grad_image_ref)

    def text_side(slot, diag=False):
        block = img[slot]
        z = sharp * product(txt[OWN], block) + shift
        e = jnp.exp(-jnp.abs(z))
        coeff = jnp.where(z >= 0, 1.0, e) / (1.0 + e)
        if diag:
            coeff = coeff - jnp.where(diagonal(), 1.0, 0.0)
        gather(coeff, block, grad_text_ref)

    def back(raw, acc):
        own, radius = unit(raw)
        grad = sharp * acc
        inner = jnp.sum(own * grad, axis=-1, keepdims=True)
        return (grad - own * inner) / radius

    def image_back():
        loss_ref[...] = loss_ref[...] * (1.0 / (STEPS * rows))
        grad_image_ref[...] = back(picture_ref[...], grad_image_ref[...])

    inner = jnp.logical_not(corner)
    early = lax.rem(y + core, 2) == 0
    late = jnp.logical_not(early)

    image_side(OWN, True)
    text_side(OWN, True)

    for c in chunks:
        wait_txt(Y, c)

        @pl.when(jnp.logical_not(skip_txt_z))
        def _():
            send_txt(Y, Z, c, 4, z_out)

        wait_img(X, c)
        send_img(X, V, c, 5, to_y)
        send_img(X, SIB_X, c, 6, to_sib)

    @pl.when(inner)
    def _():
        for c in chunks:
            send_img(OWN, Y, c, 7, to_y)

    @pl.when(corner)
    def _():
        for c in chunks:
            send_txt(Y, FAR, c, 9, to_x)

    @pl.when(early)
    def _():
        for c in chunks:
            send_txt(Y, SIB_E, c, 10, to_sib)

    for c in chunks:
        wait_txt(SIB, c)
        wait_img(SIB, c)
    image_side(SIB)
    text_side(SIB)
    text_side(X)

    for c in chunks:
        @pl.when(jnp.logical_not(skip_txt_z))
        def _():
            wait_txt(Z, c)

        @pl.when(inner)
        def _():
            send_txt(Z, FAR, c, 9, to_x)

        @pl.when(late)
        def _():
            send_txt(Z, SIB_E, c, 10, to_sib)

        @pl.when(corner)
        def _():
            wait_img(V, c)
            send_img(V, FAR, c, 11, z_out)

        @pl.when(inner)
        def _():
            wait_img(Y, c)

            @pl.when(jnp.logical_not(skip_img_z))
            def _():
                send_img(Y, Z, c, 12, z_out)

        wait_txt(X, c)
        send_txt(X, SIB_X, c, 13, to_sib)

    for c in chunks:
        wait_img(SIB_X, c)
    text_side(SIB_X)
    image_side(X)
    image_side(lax.select(y == 0, Z, Y))
    for c in chunks:
        wait_txt(SIB_E, c)
        wait_txt(SIB_X, c)
    image_side(SIB_E)
    image_side(SIB_X)

    for c in chunks:
        @pl.when(corner)
        def _():
            wait_img(Y, c)

            @pl.when(jnp.logical_not(skip_img_z))
            def _():
                send_img(Y, Z, c, 12, z_out)

            wait_img(FAR, c)
            send_img(FAR, SIB_F, c, 16, to_sib)

        @pl.when(inner)
        def _():
            wait_img(V, c)
            send_img(V, SIB_F, c, 16, to_sib)

        wait_txt(FAR, c)
        send_txt(FAR, SIB_F, c, 15, to_sib)

    @pl.when(early)
    def _():
        for c in chunks:
            send_img(Y, SIB_E, c, 14, to_sib)

    text_side(lax.select(corner, FAR, V))
    image_side(FAR)
    for c in chunks:
        wait_txt(SIB_F, c)
        wait_img(SIB_F, c)
    image_side(SIB_F)
    text_side(SIB_F)
    image_back()

    for c in chunks:
        @pl.when(jnp.logical_not(skip_img_z))
        def _():
            wait_img(Z, c)

        @pl.when(late)
        def _():
            send_img(Z, SIB_E, c, 14, to_sib)

    text_side(lax.select(y == 0, Y, Z))
    for c in chunks:
        wait_img(SIB_E, c)
    text_side(SIB_E)
    grad_text_ref[...] = back(caption_ref[...], grad_text_ref[...])

    def sent(number):
        for c in chunks:
            copy(txt, txt_sem, OWN, OWN, c, number, to_sib).wait_send()

    for number in (0, 1, 2, 3, 5, 6, 7, 8, 9, 10, 13, 14, 15, 16):
        sent(number)

    @pl.when(jnp.logical_not(skip_txt_z))
    def _():
        sent(4)

    @pl.when(corner)
    def _():
        sent(11)

    @pl.when(jnp.logical_not(skip_img_z))
    def _():
        sent(12)


def per_device_tree(picture, caption, sharpness, offset):
    rows, width = picture.shape
    vmem = pl.BlockSpec(memory_space=pltpu.VMEM)
    smem = pl.BlockSpec(memory_space=pltpu.SMEM)
    loss, grad_image, grad_text = pl.pallas_call(
        tree_kernel,
        out_shape=(
            jax.ShapeDtypeStruct((rows, 1), jnp.float32),
            jax.ShapeDtypeStruct((rows, width), jnp.float32),
            jax.ShapeDtypeStruct((rows, width), jnp.float32),
        ),
        in_specs=[vmem, vmem, smem, smem],
        out_specs=(vmem, vmem, vmem),
        scratch_shapes=[
            pltpu.VMEM((SLOTS, rows, width), jnp.bfloat16),
            pltpu.VMEM((SLOTS, rows, width), jnp.bfloat16),
            pltpu.VMEM((rows, width), jnp.bfloat16),
            pltpu.SemaphoreType.DMA((SLOTS, CHUNKS)),
            pltpu.SemaphoreType.DMA((SLOTS, CHUNKS)),
            pltpu.SemaphoreType.DMA((SENDS, CHUNKS)),
        ],
        compiler_params=pltpu.CompilerParams(
            collective_id=0, has_side_effects=True, vmem_limit_bytes=48 * 1024 * 1024
        ),
        cost_estimate=pl.CostEstimate(
            flops=14 * STEPS * rows * rows * width,
            bytes_accessed=16 * rows * width,
            transcendentals=4 * STEPS * rows * rows,
        ),
    )(picture, caption, sharpness, offset)
    return loss.reshape(rows), grad_image, grad_text


def solution(mesh):
    body = per_device_tree if mesh.shape["dp"] == 32 else per_device
    return jax.shard_map(
        body,
        mesh=mesh,
        in_specs=(P("dp", None), P("dp", None), P(), P()),
        out_specs=(P("dp"), P("dp", None), P("dp", None)),
        check_vma=False,
    )
```

```python
import functools

import jax
import jax.numpy as jnp
from jax import lax
from jax.experimental import pallas as pl
from jax.experimental.pallas import tpu as pltpu
from jax.sharding import PartitionSpec as P

STEPS = 8


epsilon = 1e-06


def shifted(value, axis, by):
    size = lax.axis_size(axis)
    return lax.ppermute(value, axis, [(i, (i + by) % size) for i in range(size)])


def unit_rows(values):
    radius = jnp.sqrt(jnp.sum(values * values, axis=-1, keepdims=True) + epsilon)
    return (values / radius, radius)


def back_rows(grad_unit, unit, radius):
    inner = jnp.sum(unit * grad_unit, axis=-1, keepdims=True)
    return (grad_unit - unit * inner) / radius


def per_device(picture_embeddings_raw, caption_embeddings_raw, sharpness_array, offset_term_array):
    row_count = picture_embeddings_raw.shape[0]
    step_total = STEPS
    half_steps = step_total // 2
    image_unit_vectors, img_radius = unit_rows(picture_embeddings_raw)
    txt_unit, txt_radius = unit_rows(caption_embeddings_raw)
    txt_send = txt_unit.astype(jnp.bfloat16)
    sharpness_multiplier = sharpness_array[0]
    additive_offset_term = offset_term_array[0]
    diagonal_ones = jnp.eye(row_count, dtype=jnp.float32)

    def labels(offset):
        if offset == 0:
            return diagonal_ones
        return jnp.zeros_like(diagonal_ones)

    chains = (-half_steps, 1, step_total)
    loss_total = jnp.zeros((row_count,), jnp.float32)
    picture_derivative_sum = jnp.zeros_like(image_unit_vectors)
    first_offset, direction, chain_steps = chains
    text_block = shifted(txt_send, "dp", -first_offset)
    carried = jnp.zeros_like(txt_unit)
    offset = first_offset
    for turn_index in range(chain_steps):
        offset = first_offset + direction * turn_index
        if turn_index > 0:
            text_block = shifted(text_block, "dp", -direction)
            carried = shifted(carried, "dp", -direction)
        neighbor_shard_index = text_block.astype(jnp.float32)
        matching_scores = (
            sharpness_multiplier
            * jnp.dot(image_unit_vectors, neighbor_shard_index.T, precision=lax.Precision.HIGHEST)
            + additive_offset_term
        )
        positive = labels(offset)
        loss_rows = jnp.sum(jax.nn.softplus(matching_scores) - positive * matching_scores, axis=1)
        match_weight_factor = jax.nn.sigmoid(matching_scores) - positive
        picture_piece = sharpness_multiplier * jnp.dot(
            match_weight_factor, neighbor_shard_index, precision=lax.Precision.HIGHEST
        )
        caption_piece = sharpness_multiplier * jnp.dot(
            match_weight_factor.T, image_unit_vectors, precision=lax.Precision.HIGHEST
        )
        loss_rows, picture_piece, caption_piece = (loss_rows, picture_piece, caption_piece)
        loss_total = loss_total + loss_rows
        picture_derivative_sum = picture_derivative_sum + picture_piece
        carried = carried + caption_piece
    text_total = shifted(carried, "dp", offset)
    row_loss = loss_total / (step_total * row_count)
    grad_image = back_rows(picture_derivative_sum, image_unit_vectors, img_radius)
    grad_text = back_rows(text_total, txt_unit, txt_radius)
    return (row_loss, grad_image, grad_text)


OWN, SIB, X, Y, Z, V, FAR, SIB_X, SIB_E, SIB_F = range(10)
SLOTS = 10
CHUNKS = 2
SENDS = 18


def tree_kernel(
    picture_ref, caption_ref, sharp_ref, offset_ref,
    loss_ref, grad_image_ref, grad_text_ref,
    txt, img, img_low, txt_sem, img_sem, send_sem,
):
    rows, width = picture_ref.shape
    part = rows // CHUNKS
    me = lax.axis_index("dp")
    total = lax.axis_size("dp")
    core = lax.rem(me, 2)
    x = lax.rem(me // 2, 2)
    y = lax.rem(me // 4, 2)
    corner = x == y
    plane = 8
    to_x = me + 2 - 4 * x
    to_y = me + 4 - 8 * y
    to_sib = me + 1 - 2 * core
    step = plane - 2 * plane * y
    z_out = lax.rem(me + step + total, total)
    z_in = lax.rem(me - step + total, total)
    skip_txt_z = jnp.logical_and(jnp.logical_and(x == 1, y == 1), core == 1)
    skip_img_z = jnp.logical_and(y == 0, core == 0)

    barrier = pltpu.get_barrier_semaphore()
    for peer in (to_x, to_y, to_sib, z_in):
        pl.semaphore_signal(barrier, inc=1, device_id=(peer,), device_id_type=pl.DeviceIdType.MESH)

    def copy(buf, sem, src, dst, chunk, number, target):
        at = pl.ds(chunk * part, part)
        return pltpu.make_async_remote_copy(
            src_ref=buf.at[src, at],
            dst_ref=buf.at[dst, at],
            send_sem=send_sem.at[number, chunk],
            recv_sem=sem.at[dst, chunk],
            device_id=(target,),
            device_id_type=pl.DeviceIdType.MESH,
        )

    def send_txt(src, dst, chunk, number, target):
        copy(txt, txt_sem, src, dst, chunk, number, target).start()

    def send_img(src, dst, chunk, number, target):
        copy(img, img_sem, src, dst, chunk, number, target).start()

    def wait_txt(dst, chunk):
        copy(txt, txt_sem, dst, dst, chunk, 0, to_sib).wait_recv()

    def wait_img(dst, chunk):
        copy(img, img_sem, dst, dst, chunk, 0, to_sib).wait_recv()

    def unit(values):
        radius = jnp.sqrt(jnp.sum(values * values, axis=-1, keepdims=True) + epsilon)
        return values / radius, radius

    chunks = range(CHUNKS)
    sharp = sharp_ref[0]
    shift = offset_ref[0]

    for c in chunks:
        at = pl.ds(c * part, part)
        txt[OWN, at] = unit(caption_ref[at])[0].astype(jnp.bfloat16)
        if c == 0:
            pl.semaphore_wait(barrier, 4)
        send_txt(OWN, Y, c, 0, to_y)
        img_unit = unit(picture_ref[at])[0]
        img_high = img_unit.astype(jnp.bfloat16)
        img[OWN, at] = img_high
        send_img(OWN, X, c, 1, to_x)
        img_low[at] = (img_unit - img_high.astype(jnp.float32)).astype(jnp.bfloat16)

    for c in chunks:
        send_txt(OWN, X, c, 8, to_x)

    @pl.when(corner)
    def _():
        for c in chunks:
            send_img(OWN, Y, c, 7, to_y)

    for c in chunks:
        send_txt(OWN, SIB, c, 2, to_sib)
        send_img(OWN, SIB, c, 3, to_sib)

    loss_ref[...] = jnp.zeros_like(loss_ref)
    grad_image_ref[...] = jnp.zeros_like(grad_image_ref)
    grad_text_ref[...] = jnp.zeros_like(grad_text_ref)

    def product(a, b):
        return lax.dot_general(a, b, (((1,), (1,)), ((), ())), preferred_element_type=jnp.float32)

    def gather(coeff, block, acc):
        high = coeff.astype(jnp.bfloat16)
        low = (coeff - high.astype(jnp.float32)).astype(jnp.bfloat16)
        acc[...] += jnp.dot(high, block, preferred_element_type=jnp.float32) + jnp.dot(
            low, block, preferred_element_type=jnp.float32
        )

    def diagonal():
        shape = (rows, rows)
        return lax.broadcasted_iota(jnp.int32, shape, 0) == lax.broadcasted_iota(jnp.int32, shape, 1)

    def image_side(slot, diag=False):
        block = txt[slot]
        z = sharp * (product(img[OWN], block) + product(img_low[...], block)) + shift
        e = jnp.exp(-jnp.abs(z))
        loss = jnp.maximum(z, 0.0) + jnp.log1p(e)
        coeff = jnp.where(z >= 0, 1.0, e) / (1.0 + e)
        if diag:
            loss = loss - jnp.where(diagonal(), z, 0.0)
            coeff = coeff - jnp.where(diagonal(), 1.0, 0.0)
        loss_ref[...] += jnp.sum(loss, axis=1, keepdims=True)
        grad_image_ref[...] += jnp.dot(coeff.astype(jnp.bfloat16), block, preferred_element_type=jnp.float32)

    def text_side(slot, diag=False):
        block = img[slot]
        z = sharp * product(txt[OWN], block) + shift
        e = jnp.exp(-jnp.abs(z))
        coeff = jnp.where(z >= 0, 1.0, e) / (1.0 + e)
        if diag:
            coeff = coeff - jnp.where(diagonal(), 1.0, 0.0)
        gather(coeff, block, grad_text_ref)

    def back(raw, acc):
        own, radius = unit(raw)
        grad = sharp * acc
        inner = jnp.sum(own * grad, axis=-1, keepdims=True)
        return (grad - own * inner) / radius

    def image_back():
        loss_ref[...] = loss_ref[...] * (1.0 / (STEPS * rows))
        grad_image_ref[...] = back(picture_ref[...], grad_image_ref[...])

    inner = jnp.logical_not(corner)
    early = lax.rem(y + core, 2) == 0
    late = jnp.logical_not(early)

    image_side(OWN, True)
    text_side(OWN, True)

    for c in chunks:
        wait_txt(Y, c)

        @pl.when(jnp.logical_not(skip_txt_z))
        def _():
            send_txt(Y, Z, c, 4, z_out)

        wait_img(X, c)
        send_img(X, V, c, 5, to_y)
        send_img(X, SIB_X, c, 6, to_sib)

    @pl.when(inner)
    def _():
        for c in chunks:
            send_img(OWN, Y, c, 7, to_y)

    @pl.when(corner)
    def _():
        for c in chunks:
            send_txt(Y, FAR, c, 9, to_x)

    @pl.when(early)
    def _():
        for c in chunks:
            send_txt(Y, SIB_E, c, 10, to_sib)

    for c in chunks:
        wait_txt(SIB, c)
        wait_img(SIB, c)
    image_side(SIB)
    text_side(SIB)
    text_side(X)

    for c in chunks:
        @pl.when(jnp.logical_not(skip_txt_z))
        def _():
            wait_txt(Z, c)

        @pl.when(inner)
        def _():
            send_txt(Z, FAR, c, 9, to_x)

        @pl.when(late)
        def _():
            send_txt(Z, SIB_E, c, 10, to_sib)

        @pl.when(corner)
        def _():
            wait_img(V, c)
            send_img(V, FAR, c, 11, z_out)

        @pl.when(inner)
        def _():
            wait_img(Y, c)

            @pl.when(jnp.logical_not(skip_img_z))
            def _():
                send_img(Y, Z, c, 12, z_out)

        wait_txt(X, c)
        send_txt(X, SIB_X, c, 13, to_sib)

    for c in chunks:
        wait_img(SIB_X, c)
    text_side(SIB_X)
    image_side(X)
    image_side(lax.select(y == 0, Z, Y))
    for c in chunks:
        wait_txt(SIB_E, c)
        wait_txt(SIB_X, c)
    image_side(SIB_E)
    image_side(SIB_X)

    for c in chunks:
        @pl.when(corner)
        def _():
            wait_img(Y, c)

            @pl.when(jnp.logical_not(skip_img_z))
            def _():
                send_img(Y, Z, c, 12, z_out)

            wait_img(FAR, c)
            send_img(FAR, SIB_F, c, 16, to_sib)

        @pl.when(inner)
        def _():
            wait_img(V, c)
            send_img(V, SIB_F, c, 16, to_sib)

        wait_txt(FAR, c)
        send_txt(FAR, SIB_F, c, 15, to_sib)

    @pl.when(early)
    def _():
        for c in chunks:
            send_img(Y, SIB_E, c, 14, to_sib)

    text_side(lax.select(corner, FAR, V))
    image_side(FAR)
    for c in chunks:
        wait_txt(SIB_F, c)
        wait_img(SIB_F, c)
    image_side(SIB_F)
    text_side(SIB_F)
    image_back()

    for c in chunks:
        @pl.when(jnp.logical_not(skip_img_z))
        def _():
            wait_img(Z, c)

        @pl.when(late)
        def _():
            send_img(Z, SIB_E, c, 14, to_sib)

    text_side(lax.select(y == 0, Y, Z))
    for c in chunks:
        wait_img(SIB_E, c)
    text_side(SIB_E)
    grad_text_ref[...] = back(caption_ref[...], grad_text_ref[...])

    def sent(number):
        for c in chunks:
            copy(txt, txt_sem, OWN, OWN, c, number, to_sib).wait_send()

    for number in (0, 1, 2, 3, 5, 6, 7, 8, 9, 10, 13, 14, 15, 16):
        sent(number)

    @pl.when(jnp.logical_not(skip_txt_z))
    def _():
        sent(4)

    @pl.when(corner)
    def _():
        sent(11)

    @pl.when(jnp.logical_not(skip_img_z))
    def _():
        sent(12)


def per_device_tree(picture, caption, sharpness, offset):
    rows, width = picture.shape
    vmem = pl.BlockSpec(memory_space=pltpu.VMEM)
    smem = pl.BlockSpec(memory_space=pltpu.SMEM)
    loss, grad_image, grad_text = pl.pallas_call(
        tree_kernel,
        out_shape=(
            jax.ShapeDtypeStruct((rows, 1), jnp.float32),
            jax.ShapeDtypeStruct((rows, width), jnp.float32),
            jax.ShapeDtypeStruct((rows, width), jnp.float32),
        ),
        in_specs=[vmem, vmem, smem, smem],
        out_specs=(vmem, vmem, vmem),
        scratch_shapes=[
            pltpu.VMEM((SLOTS, rows, width), jnp.bfloat16),
            pltpu.VMEM((SLOTS, rows, width), jnp.bfloat16),
            pltpu.VMEM((rows, width), jnp.bfloat16),
            pltpu.SemaphoreType.DMA((SLOTS, CHUNKS)),
            pltpu.SemaphoreType.DMA((SLOTS, CHUNKS)),
            pltpu.SemaphoreType.DMA((SENDS, CHUNKS)),
        ],
        compiler_params=pltpu.CompilerParams(
            collective_id=0, has_side_effects=True, vmem_limit_bytes=48 * 1024 * 1024
        ),
        cost_estimate=pl.CostEstimate(
            flops=14 * STEPS * rows * rows * width,
            bytes_accessed=16 * rows * width,
            transcendentals=4 * STEPS * rows * rows,
        ),
    )(picture, caption, sharpness, offset)
    return loss.reshape(rows), grad_image, grad_text


def solution(mesh):
    body = per_device_tree if mesh.shape["dp"] == 32 else per_device
    return jax.shard_map(
        body,
        mesh=mesh,
        in_specs=(P("dp", None), P("dp", None), P(), P()),
        out_specs=(P("dp"), P("dp", None), P("dp", None)),
        check_vma=False,
    )
```
